512 devices in a mesh: group: 8 (over x, core), dev: 64 (over z, y).
Axes of the slice: x: 4, y: 8, z: 8, core: 2. Of those that a mesh axis runs over, the one named last changes fastest.
Arguments:
- positions: float32 [3, 16777216], P(None, ('group', 'dev')), may hold values from -1 to 1
- strengths: float32 [3, 16777216], P(None, ('group', 'dev')), may hold values from -0.6 to 0.6
- active: int32 [131072], P(('group', 'dev')), may hold values from 0 to 1, as said below
- m2l_list: int32 [512, 3, 1152], P(('group', 'dev')), may hold values from -1 to 255, as said below
- p2p_list: int32 [512, 3, 128], P(('group', 'dev')), may hold values from -1 to 255, as said below
- local_pairs: int32 [512, 3, 128], P(('group', 'dev')), may hold values from -1 to 255, as said below
- m2l_ops: bfloat16 [32, 128, 128], replicated, may hold values from -3 to 3
Outputs:
- field: float32 [3, 16777216], P(None, ('group', 'dev'))
The draws below stay inside these ranges and needn't reach their ends.
Inputs may be any that keep to these rules, and one draw needn't show every extreme that they name: Each device's 256 leaves hold between 4 and 32 active leaves; some device holds exactly 32. `m2l_list`: device (g, d), column b * 128 + c with b = 3 (i + 1) + (k + 1) for i, k in -1, 0, 1: row 0 is a leaf of device (g, d), row 1 an offset class below 32 equal to 8 - b modulo 9, row 2 an active leaf of device (g + i, d + k); or -1, 0, -1 in an empty column. Blocks towards positions outside the mesh are empty. Every active leaf is the target of exactly one slot of each offset class whose source position lies in the mesh. `p2p_list`: device (g, d), column j * 32 + c with (i, k) = (-1, -1), (-1, 0), (-1, 1), (0, -1) for j = 0, 1, 2, 3: rows 0 and 1 are active leaves of device (g, d) and of device (g + i, d + k), row 2 a neighbour class below 26; or -1, -1, 0 in an empty column. Blocks towards positions outside the mesh are empty. `local_pairs`: rows 0 and 1 are two different active leaves of the device, row 2 a neighbour class below 26; a device with k active leaves has live pairs in its first 4 k columns and -1, -1, 0 in the rest.
All inputs are finite; a program needn't handle non-finite values.
Results may differ from the reference program's by a relative error of at most 0.0013.
Values may be sent and summed in bfloat16 or wider, within the bound.
No kernel may reach another device: no remote copies, remote signals or barrier semaphores. Data moves between devices by JAX's collectives and lax.ppermute only.
A program may use at most 64 MiB of HBM per device.

```python
import math
import jax
import jax.numpy as jnp
from jax import lax

LEAF_PART = 128
COEF = 128
ORDER = 5
OFFSETS = 32
LEAF_DEV = 256
ACT_MOST = 32
M2L_CAP = 128
PCAP = 32
LOCAL_CAP = 128
PARTS_SIZE = 16777216
N_GROUP = 8
N_DEV = 64
DEVICES = 512


FORWARD_GROUP = (-1, -1, -1, 0)


FORWARD_MEMBER = (-1, 0, 1, -1)


def activity(key):
    first, second, third, fourth, fifth = jax.random.split(key, 5)
    product = jax.random.randint(first, (DEVICES,), 0, ACT_MOST + 1) * jax.random.randint(second, (DEVICES,), 0, ACT_MOST + 1)
    counts = jnp.maximum(product // ACT_MOST, ACT_MOST // 8)
    busy_group = 1 + jax.random.randint(third, (), 0, N_GROUP - 1)
    busy_member = 1 + jax.random.randint(fifth, (), 0, N_DEV - 1)
    busiest = busy_group * N_DEV + busy_member
    counts = jnp.where(jnp.arange(DEVICES) == busiest, ACT_MOST, counts).astype(jnp.int32)
    orders = jax.vmap(lambda sub: jax.random.permutation(sub, LEAF_DEV))(jax.random.split(fourth, DEVICES)).astype(jnp.int32)
    return (counts, orders)


def neighbours(steps_group, steps_member):
    device = jnp.arange(DEVICES)
    to_group = (device // N_DEV)[:, None] + steps_group[None, :]
    to_member = (device % N_DEV)[:, None] + steps_member[None, :]
    inside = (to_group >= 0) & (to_group < N_GROUP) & (to_member >= 0) & (to_member < N_DEV)
    return (inside, jnp.where(inside, to_group * N_DEV + to_member, 0))


def draw_active(key, part):
    counts, orders = activity(key)
    key = jax.random.fold_in(key, 5)
    live = (jnp.arange(LEAF_DEV)[None, :] < counts[:, None]).astype(jnp.int32)
    flags = jnp.zeros((DEVICES, LEAF_DEV), jnp.int32).at[jnp.arange(DEVICES)[:, None], orders].set(live)
    return flags.reshape(-1)


def draw_m2l_list(key, part):
    counts, orders = activity(key)
    key = jax.random.fold_in(key, 11)
    first, second = jax.random.split(key)
    directions = jnp.arange(9)
    inside, receiver = neighbours(directions // 3 - 1, directions % 3 - 1)
    residue = 8 - directions
    per_class = (OFFSETS - residue + 8) // 9
    ranks = jax.vmap(lambda sub: jax.random.permutation(sub, M2L_CAP))(jax.random.split(first, DEVICES * 9)).reshape(DEVICES, 9, M2L_CAP)
    live = inside[:, :, None] & (ranks < (counts[receiver] * per_class[None, :])[:, :, None])
    leaf_rank = jnp.clip(ranks // per_class[None, :, None], 0, LEAF_DEV - 1)
    offset = residue[None, :, None] + 9 * (ranks % per_class[None, :, None])
    target = orders[receiver[:, :, None], leaf_rank]
    source = jax.random.randint(second, (DEVICES, 9, M2L_CAP), 0, LEAF_DEV)
    rows = [jnp.where(live, source, -1), jnp.where(live, offset, 0), jnp.where(live, target, -1)]
    return jnp.stack(rows, axis=1).reshape(DEVICES, 3, 9 * M2L_CAP).astype(jnp.int32)


def draw_p2p_list(key, part):
    counts, orders = activity(key)
    key = jax.random.fold_in(key, 23)
    first, second = jax.random.split(key)
    inside, receiver = neighbours(jnp.array(FORWARD_GROUP), jnp.array(FORWARD_MEMBER))
    column = jnp.arange(PCAP)
    live = inside[:, :, None] & (column[None, None, :] < counts[:, None, None])
    leaf_first = jnp.broadcast_to(orders[:, :PCAP][:, None, :], (DEVICES, 4, PCAP))
    pick = jax.random.randint(first, (DEVICES, 4, PCAP), 0, LEAF_DEV) % counts[receiver][:, :, None]
    leaf_second = orders[receiver[:, :, None], pick]
    codes = jax.random.randint(second, (DEVICES, 4, PCAP), 0, 26)
    rows = [jnp.where(live, leaf_first, -1), jnp.where(live, leaf_second, -1), jnp.where(live, codes, 0)]
    return jnp.stack(rows, axis=1).reshape(DEVICES, 3, 4 * PCAP).astype(jnp.int32)


def draw_local_pairs(key, part):
    counts, orders = activity(key)
    key = jax.random.fold_in(key, 37)
    first, second, third = jax.random.split(key, 3)
    live = jnp.arange(LOCAL_CAP)[None, :] < 4 * counts[:, None]
    pick_first = jax.random.randint(first, (DEVICES, LOCAL_CAP), 0, LEAF_DEV) % counts[:, None]
    stride = 1 + jax.random.randint(second, (DEVICES, LOCAL_CAP), 0, LEAF_DEV) % (counts[:, None] - 1)
    pick_second = (pick_first + stride) % counts[:, None]
    leaf_first = jnp.take_along_axis(orders, pick_first, axis=1)
    leaf_second = jnp.take_along_axis(orders, pick_second, axis=1)
    codes = jax.random.randint(third, (DEVICES, LOCAL_CAP), 0, 26)
    leaf_first = jnp.where(live, leaf_first, -1)
    leaf_second = jnp.where(live, leaf_second, -1)
    codes = jnp.where(live, codes, 0)
    return jnp.stack([leaf_first, leaf_second, codes], axis=1).astype(jnp.int32)


def level_of(key, dims, cuts, smallest, high):
    def one(position, blocks):
        draws = jax.random.uniform(jax.random.fold_in(jax.random.fold_in(key, 6), position), (blocks,), jnp.float32, smallest / len(cuts), high / len(cuts))
        return jnp.repeat(jnp.exp(draws), dims[position] // blocks).reshape((-1,) + (1,) * (len(dims) - position - 1))

    factor_of = one(*cuts[0])
    for cut in cuts[1:]:
        factor_of = factor_of * one(*cut)
    return factor_of


def scatter_about(rng, shape, scale, limit, cuts=(), kind=jnp.bfloat16):
    entries = jax.random.normal(rng, shape, jnp.float32) * scale
    if len(cuts) > 0:
        entries = level_of(rng, shape, cuts, -0.22, 0.18) * entries
    return jnp.clip(entries, min=-limit, max=limit).astype(kind)


def setup_inputs(seed: int = 0) -> dict:
    key_list = jax.random.split(jax.random.key(seed), 8)
    positions = jnp.clip(jax.random.uniform(key_list[0], (3, PARTS_SIZE), jnp.float32, -1.0, 1.0) * level_of(key_list[0], (3, PARTS_SIZE), ((1, 512),), -0.4, 0.0), -1.0, 1.0)
    strengths = scatter_about(key_list[1], (3, PARTS_SIZE), 0.1, 0.6, ((1, 512),), jnp.float32)
    active = draw_active(jax.random.fold_in(key_list[7], 71), 0)
    m2l_list = draw_m2l_list(jax.random.fold_in(key_list[7], 71), 0)
    p2p_list = draw_p2p_list(jax.random.fold_in(key_list[7], 71), 0)
    local_pairs = draw_local_pairs(jax.random.fold_in(key_list[7], 71), 0)
    m2l_ops = scatter_about(key_list[6], (OFFSETS, COEF, COEF), 0.5, 3.0)
    return {"positions": positions, "strengths": strengths, "active": active, "m2l_list": m2l_list, "p2p_list": p2p_list, "local_pairs": local_pairs, "m2l_ops": m2l_ops}


SMOOTH = 0.04
FORWARD_GROUP = (-1, -1, -1, 0)
FORWARD_MEMBER = (-1, 0, 1, -1)

def cheb_basis(coords, points, columns):
    angles = (2.0 * jnp.arange(points, dtype=jnp.float32) + 1.0) * (math.pi / (2.0 * points))
    degrees = jnp.arange(points, dtype=jnp.float32)
    table = jnp.cos(degrees[:, None] * angles[None, :])

    def one_dimension(values):
        previous = jnp.ones_like(values)
        current = values
        total = jnp.zeros(values.shape + (points,), jnp.float32) + 1.0 / points
        for degree in range(1, points):
            total = total + 2.0 / points * current[..., None] * table[degree]
            previous, current = (current, 2.0 * values * current - previous)
        return total
    along_x = one_dimension(coords[0])
    along_y = one_dimension(coords[1])
    along_z = one_dimension(coords[2])
    joint = along_x[..., :, None, None] * along_y[..., None, :, None] * along_z[..., None, None, :]
    joint = joint.reshape(coords.shape[1:] + (points ** 3,))
    padding = [(0, 0)] * (joint.ndim - 1) + [(0, columns - points ** 3)]
    return jnp.pad(joint, padding)

def multipoles(leaf_pos, leaf_str):
    count = leaf_pos.shape[1]
    width = math.gcd(count, 32)

    def one_block(pieces):
        block_pos, block_str = pieces
        basis = cheb_basis(block_pos, ORDER, COEF)
        return jnp.einsum('clp,lpn->lcn', block_str, basis, precision=lax.Precision.HIGHEST)

    def regroup(array):
        return jnp.moveaxis(array.reshape((3, count // width, width) + array.shape[2:]), 1, 0)
    result = lax.map(one_block, (regroup(leaf_pos), regroup(leaf_str)))
    return result.reshape(count, 3, COEF).astype(jnp.bfloat16)

def displacement(codes):
    shifted = codes + (codes >= 13).astype(jnp.int32)
    return jnp.stack([shifted // 9 - 1, shifted // 3 % 3 - 1, shifted % 3 - 1]).astype(jnp.float32)

def kernel_block(pos_left, pos_right, shift):
    pieces = [shift[component][:, None, None] + 0.5 * (pos_right[component][:, None, :] - pos_left[component][:, :, None]) for component in range(3)]
    return lax.rsqrt(pieces[0] * pieces[0] + pieces[1] * pieces[1] + pieces[2] * pieces[2] + SMOOTH)

def pair_terms(pos_left, str_left, pos_right, str_right, shift, want_left, want_right):
    count = pos_left.shape[1]
    block = math.gcd(count, 32)
    blocks = count // block

    def regroup(array):
        return jnp.moveaxis(array.reshape((array.shape[0], blocks, block) + array.shape[2:]), 1, 0)

    def one_block(pieces):
        left_pos, left_str, right_pos, right_str, offset = pieces
        kernel = kernel_block(left_pos, right_pos, offset)
        results = []
        if want_left:
            results.append(jnp.einsum('cpj,pij->cpi', right_str, kernel, precision=lax.Precision.HIGHEST))
        if want_right:
            results.append(jnp.einsum('cpi,pij->cpj', left_str, kernel, precision=lax.Precision.HIGHEST))
        return tuple(results)
    outputs = lax.map(one_block, (regroup(pos_left), regroup(str_left), regroup(pos_right), regroup(str_right), regroup(shift)))
    return tuple((jnp.moveaxis(piece_out, 0, 1).reshape((3, count) + piece_out.shape[3:]) for piece_out in outputs))

def compact(flags, most):
    leaf_count = flags.shape[0]
    ranking = (jnp.cumsum(flags) - 1).astype(jnp.int32)
    chosen = (ranking[None, :] == jnp.arange(most, dtype=jnp.int32)[:, None]) & (flags[None, :] == 1)
    active_index = lax.optimization_barrier(jnp.sum(jnp.where(chosen, jnp.arange(leaf_count, dtype=jnp.int32)[None, :], 0), axis=1)).astype(jnp.int32)
    active_live = jnp.any(chosen, axis=1).astype(jnp.float32)
    slot_of_leaf = jnp.where(flags == 1, ranking, most).astype(jnp.int32)
    return (active_index, active_live, slot_of_leaf)

def gather_leaves(leaf_pos, leaf_str, index):
    live = (index >= 0).astype(jnp.float32)
    safe = jnp.clip(index, 0, leaf_pos.shape[1] - 1).astype(jnp.int32)
    return (jnp.take(leaf_pos, safe, axis=1), jnp.take(leaf_str, safe, axis=1) * live[None, :, None])

def reference(positions, strengths, active, m2l_list, p2p_list, local_pairs, m2l_ops):
    leaf_total = DEVICES * LEAF_DEV
    leaf_pos = positions.reshape(3, leaf_total, LEAF_PART)
    leaf_str = strengths.reshape(3, leaf_total, LEAF_PART)
    device_ids = jnp.arange(DEVICES, dtype=jnp.int32)

    def expand(device):
        start = device * LEAF_DEV
        return multipoles(lax.dynamic_slice_in_dim(leaf_pos, start, LEAF_DEV, 1), lax.dynamic_slice_in_dim(leaf_str, start, LEAF_DEV, 1))
    moments = lax.map(expand, device_ids).reshape(leaf_total, 3, COEF)
    wide_ops = m2l_ops.astype(jnp.float32)
    directions = jnp.arange(9, dtype=jnp.int32)
    block_group = directions // 3 - 1
    block_member = directions % 3 - 1

    def device_field(device):
        start = device * LEAF_DEV
        flags = lax.dynamic_slice_in_dim(active, start, LEAF_DEV, 0)
        active_index, active_live, slot_of_leaf = compact(flags, ACT_MOST)
        own_pos = lax.dynamic_slice_in_dim(leaf_pos, start, LEAF_DEV, 1)
        own_str = lax.dynamic_slice_in_dim(leaf_str, start, LEAF_DEV, 1)
        active_pos = jnp.take(own_pos, active_index, axis=1)
        active_str = jnp.take(own_str, active_index, axis=1) * active_live[None, :, None]
        self_field, = pair_terms(active_pos, active_str, active_pos, active_str, jnp.zeros((3, ACT_MOST), jnp.float32), True, False)
        my_group = device // N_DEV
        my_member = device % N_DEV
        sender_group = my_group - block_group
        sender_member = my_member - block_member
        inside = (sender_group >= 0) & (sender_group < N_GROUP) & (sender_member >= 0) & (sender_member < N_DEV)
        senders = jnp.where(inside, sender_group * N_DEV + sender_member, 0).astype(jnp.int32)
        columns = m2l_list[senders].reshape(9, 3, 9, M2L_CAP)
        received = jnp.stack([columns[direction, :, direction] for direction in range(9)])
        sources = jnp.where(received[:, 0] >= 0, senders[:, None] * LEAF_DEV + received[:, 0], 0).reshape(-1).astype(jnp.int32)
        classes = received[:, 1].reshape(-1).astype(jnp.int32)
        targets = jnp.where(inside[:, None], received[:, 2], -1).reshape(-1).astype(jnp.int32)
        target_slot = jnp.where(targets >= 0, slot_of_leaf[jnp.maximum(targets, 0)], ACT_MOST).astype(jnp.int32)
        grid = jnp.zeros((ACT_MOST + 1, OFFSETS, 3, COEF), jnp.float32).at[target_slot, classes].add(moments[sources].astype(jnp.float32))
        local_exp = jnp.einsum('tock,okj->tcj', grid[:ACT_MOST], wide_ops, precision=lax.Precision.HIGHEST)
        far_basis = cheb_basis(active_pos, ORDER, COEF)
        far_field = jnp.einsum('tcn,tpn->ctp', local_exp, far_basis, precision=lax.Precision.HIGHEST) * active_live[None, :, None]
        slots = jnp.where(active_live > 0, active_index, LEAF_DEV).astype(jnp.int32)
        return jnp.zeros((3, LEAF_DEV + 1, LEAF_PART), jnp.float32).at[:, slots].add(self_field + far_field)[:, :LEAF_DEV]
    fields = lax.map(device_field, device_ids)
    fields = jnp.moveaxis(fields, 0, 1).reshape(3, leaf_total, LEAF_PART)
    step_group = jnp.array(FORWARD_GROUP, dtype=jnp.int32)
    step_member = jnp.array(FORWARD_MEMBER, dtype=jnp.int32)
    to_group = (device_ids // N_DEV)[:, None] + step_group[None, :]
    to_member = (device_ids % N_DEV)[:, None] + step_member[None, :]
    inside = (to_group >= 0) & (to_group < N_GROUP) & (to_member >= 0) & (to_member < N_DEV)
    receivers = jnp.where(inside, to_group * N_DEV + to_member, 0).astype(jnp.int32)
    pair_first = p2p_list[:, 0].reshape(DEVICES, 4, PCAP)
    pair_second = p2p_list[:, 1].reshape(DEVICES, 4, PCAP)
    remote_first = jnp.where(pair_first >= 0, device_ids[:, None, None] * LEAF_DEV + pair_first, -1)
    remote_second = jnp.where((pair_second >= 0) & inside[:, :, None], receivers[:, :, None] * LEAF_DEV + pair_second, -1)
    local_first = jnp.where(local_pairs[:, 0] >= 0, device_ids[:, None] * LEAF_DEV + local_pairs[:, 0], -1)
    local_second = jnp.where(local_pairs[:, 1] >= 0, device_ids[:, None] * LEAF_DEV + local_pairs[:, 1], -1)
    firsts = jnp.concatenate([remote_first.reshape(-1), local_first.reshape(-1)]).astype(jnp.int32)
    seconds = jnp.concatenate([remote_second.reshape(-1), local_second.reshape(-1)]).astype(jnp.int32)
    codes = jnp.concatenate([p2p_list[:, 2].reshape(-1), local_pairs[:, 2].reshape(-1)]).astype(jnp.int32)
    block = 256
    padding = -firsts.shape[0] % block
    firsts = jnp.pad(firsts, (0, padding), constant_values=-1)
    seconds = jnp.pad(seconds, (0, padding), constant_values=-1)
    codes = jnp.pad(codes, (0, padding))

    def accumulate(total, pieces):
        first, second, code = pieces
        first_pos, first_str = gather_leaves(leaf_pos, leaf_str, first)
        second_pos, second_str = gather_leaves(leaf_pos, leaf_str, second)
        to_first, to_second = pair_terms(first_pos, first_str, second_pos, second_str, displacement(code), True, True)
        total = total.at[:, jnp.where(first >= 0, first, leaf_total)].add(to_first)
        total = total.at[:, jnp.where(second >= 0, second, leaf_total)].add(to_second)
        return (total, None)
    near_field, unused = lax.scan(accumulate, jnp.zeros((3, leaf_total + 1, LEAF_PART), jnp.float32), (firsts.reshape(-1, block), seconds.reshape(-1, block), codes.reshape(-1, block)))
    total = fields + near_field[:, :leaf_total]
    return total.reshape(3, PARTS_SIZE)
```

```python
import math

import jax
import jax.numpy as jnp
import ml_dtypes
import numpy as np
from jax import lax
from jax.experimental import pallas as pl
from jax.experimental.pallas import tpu as pltpu
from jax.sharding import PartitionSpec as P

COEF = 128
ORDER = 5
OFFSETS = 32
ACT_MOST = 32
LEAF_PART = 128
LEAF_DEV = 256
PCAP = 32
DEAD = ACT_MOST
ROWS_LEAF = 6
META = ROWS_LEAF * ACT_MOST
PACKET = META + 8
GROUP_LEAVES = 8
PAIRS = 16
FIRST = 4
SMOOTH = 0.04
FORWARD_GROUP = (-1, -1, -1, 0)
FORWARD_MEMBER = (-1, 0, 1, -1)
VMEM_LIMIT = 40 * 1024 * 1024

F32 = jnp.float32
BF16 = jnp.bfloat16
NT = (((1,), (1,)), ((), ()))
NN = (((1,), (0,)), ((), ()))


def dot(left, right, dims=NN):
    return lax.dot_general(left, right, dims, preferred_element_type=F32)


def split(value):
    high = value.astype(BF16)
    return high, (value - high.astype(F32)).astype(BF16)


def iota(shape, dim):
    return lax.broadcasted_iota(jnp.int32, shape, dim)


def combination(rows):
    table = np.zeros((len(rows), 32), np.float64)
    for at, row in enumerate(rows):
        if row is None:
            continue
        raw, point = row
        if point is None:
            table[at, raw] = 1.0
            continue
        table[at, 6] = 1.0 / ORDER
        for degree in range(1, ORDER):
            angle = degree * (2 * point + 1) * math.pi / (2 * ORDER)
            table[at, 8 * (degree - 1) + raw] = 2.0 / ORDER * math.cos(angle)
    high = table.astype(ml_dtypes.bfloat16)
    low = (table - high.astype(np.float64)).astype(ml_dtypes.bfloat16)
    return np.concatenate([high, high, low], axis=1)


def moment_rows():
    points = range(ORDER)
    along_x = [(0, a) for c in range(3) for a in points] + [None]
    strength = [(3 + c, None) for c in range(3) for a in points] + [None]
    along_y = [(1, b) for b in points for g in points] + [None] * 7
    along_z = [(2, g) for b in points for g in points] + [None] * 7
    return combination(along_x + strength + along_y + along_z)


def basis_rows():
    points = range(ORDER)
    every = [(a, b, g) for a in points for b in points for g in points]
    return combination(
        [(dim, n[dim]) if n is not None else None for dim in range(3) for n in every + [None] * 3]
    )


def spreading():
    table = np.zeros((ORDER, 32, COEF), np.float32)
    for a in range(ORDER):
        for bg in range(ORDER**2):
            table[a, bg, a * ORDER**2 + bg] = 1.0
    return table.astype(ml_dtypes.bfloat16)


def displacements():
    table = np.zeros((2, 32, 8, LEAF_PART), np.float32)
    for code in range(26):
        shifted = code + (1 if code >= 13 else 0)
        vector = (shifted // 9 - 1, shifted // 3 % 3 - 1, shifted % 3 - 1)
        for dim in range(3):
            table[0, code, dim] = vector[dim]
            table[1, code, dim] = -vector[dim]
    return table.reshape(64, 8, LEAF_PART)


def features(raw):
    second = 2.0 * raw * raw - 1.0
    third = 2.0 * raw * second - raw
    fourth = 2.0 * raw * third - second
    high, low = split(jnp.concatenate([raw, second, third, fourth], axis=0))
    return jnp.concatenate([high, low, high], axis=0)


def presence(targets, classes, residue):
    leaves = iota((LEAF_DEV, 128), 0)
    hit = (leaves == targets).astype(F32).astype(BF16)
    counted = jnp.broadcast_to((classes == residue) & (targets >= 0), (16, 128))
    return dot(counted.astype(F32).astype(BF16), hit, NT).astype(BF16)


def below(targets):
    return (iota((LEAF_DEV, 128), 0) < targets).astype(F32).astype(BF16)


def pack_kernel(
    flags_ref, pos_ref, str_ref, active_ref, far_ref, near_ref, local_ref, packet_ref, lists_ref, index_ref
):
    def enter(leaf, count):
        index_ref[count] = leaf
        return count + flags_ref[leaf]

    for slot in range(ACT_MOST):
        index_ref[slot] = 0
    count = lax.fori_loop(0, LEAF_DEV, enter, 0, unroll=8)
    index_ref[ACT_MOST] = count
    for slot in range(ACT_MOST):
        leaf = index_ref[slot]
        leaf = jnp.where(slot < count, leaf, 0)
        here = pl.ds(pl.multiple_of(leaf * LEAF_PART, LEAF_PART), LEAF_PART)
        packet_ref[ROWS_LEAF * slot : ROWS_LEAF * slot + 3, :] = pos_ref[:, here]
        packet_ref[ROWS_LEAF * slot + 3 : ROWS_LEAF * slot + 6, :] = str_ref[:, here]

    own = jnp.broadcast_to(active_ref[...].astype(F32), (16, LEAF_DEV)).astype(BF16)

    def own_slot(row):
        rank = dot(own, below(row))[0:1]
        return jnp.where(row >= 0, rank.astype(jnp.int32), DEAD)

    second = near_ref[1:2, :]
    under = below(second)
    lanes = iota((1, 128), 1)
    second_slot = jnp.full((1, 128), DEAD, jnp.int32)
    for side in range(4):
        direction = 3 * (FORWARD_GROUP[side] + 1) + FORWARD_MEMBER[side] + 1
        there = presence(far_ref[18 + direction : 19 + direction, :], far_ref[9 + direction : 10 + direction, :], 8 - direction)
        rank = dot(there, under)[0:1].astype(jnp.int32)
        mine = (lanes >= side * PCAP) & (lanes < (side + 1) * PCAP) & (second >= 0)
        second_slot = jnp.where(mine, rank, second_slot)
    first_slot = own_slot(near_ref[0:1, :])
    codes = near_ref[2:3, :]
    lists_ref[0:1, :] = own_slot(local_ref[0:1, :])
    lists_ref[1:2, :] = own_slot(local_ref[1:2, :])
    lists_ref[2:3, :] = local_ref[2:3, :]
    lists_ref[3:4, :] = first_slot
    lists_ref[4:5, :] = second_slot
    lists_ref[5:6, :] = codes
    lists_ref[6:8, :] = jnp.zeros((2, 128), jnp.int32)
    packet_ref[META : META + 1, :] = first_slot.astype(F32)
    packet_ref[META + 1 : META + 2, :] = second_slot.astype(F32)
    packet_ref[META + 2 : META + 3, :] = codes.astype(F32)
    packet_ref[META + 3 :, :] = jnp.zeros((5, 128), F32)


def far_kernel(
    pos_ref, str_ref, far_ref, ops_ref, mix_ref, spread_ref, *rest
):
    outs, (cell_ref, moment_ref, pick_ref, place_ref, got_ref) = rest[:3], rest[3:]
    empty = jnp.zeros((7, 128), jnp.int32)
    classes = far_ref[9:18, :]
    targets = far_ref[18:27, :]
    residues = 8 - iota((9, 128), 0)
    counted = jnp.where((classes == residues) & (targets >= 0), targets, LEAF_DEV)
    counted = jnp.concatenate([counted, empty], axis=0).astype(F32).T
    sources = jnp.concatenate([far_ref[0:9, :], empty], axis=0).astype(F32).T
    leaves = iota((128, LEAF_DEV), 1).astype(F32)
    for direction in range(9):
        target = targets[direction : direction + 1]
        less = counted[:, direction : direction + 1] < target.astype(F32)
        rank = jnp.sum(jnp.where(less, 1.0, 0.0), axis=0, keepdims=True).astype(jnp.int32)
        kind = classes[direction : direction + 1]
        step = (kind >= 9).astype(jnp.int32) + (kind >= 18).astype(jnp.int32) + (kind >= 27).astype(jnp.int32)
        key = jnp.where(target >= 0, step * ACT_MOST + rank, -1)
        rows = slice(direction * 128, (direction + 1) * 128)
        place_ref[rows, :] = (iota((128, 128), 0) == key).astype(F32).astype(BF16)
        pick_ref[rows, :] = (sources[:, direction : direction + 1] == leaves).astype(F32).astype(BF16)

    mix = mix_ref[...]
    width = GROUP_LEAVES * LEAF_PART
    lane_leaf = iota((32, 128), 1) // 16

    def parts(value):
        return [value[:, leaf * LEAF_PART : (leaf + 1) * LEAF_PART] for leaf in range(GROUP_LEAVES)]

    def expand(block, carry):
        here = pl.ds(pl.multiple_of(block * width, width), width)
        raw = jnp.concatenate(
            [pos_ref[:, here], str_ref[:, here], jnp.ones((1, width), F32), jnp.zeros((1, width), F32)], axis=0
        )
        mixed = dot(mix, features(raw))
        left = jnp.concatenate(parts(mixed[0:16] * mixed[16:32]), axis=0).T
        left_high, left_low = split(left)
        right_high, right_low = split(mixed[32:64] * mixed[64:96])
        right_high = jnp.concatenate(parts(right_high), axis=0)
        right_low = jnp.concatenate(parts(right_low), axis=0)
        every = dot(
            jnp.concatenate([right_high, right_high, right_low], axis=1),
            jnp.concatenate([left_high, left_low, left_high], axis=0),
        )
        cells = every[0:32]
        for leaf in range(1, GROUP_LEAVES):
            cells = jnp.where(lane_leaf == leaf, every[32 * leaf : 32 * leaf + 32], cells)
        cell_ref[pl.ds(pl.multiple_of(block * 128, 128), 128), :] = cells.T
        return carry

    lax.fori_loop(0, LEAF_DEV // GROUP_LEAVES, expand, 0, unroll=2)
    for c in range(3):
        total = jnp.zeros((LEAF_DEV, COEF), F32)
        for a in range(ORDER):
            piece = cell_ref[pl.ds(c * ORDER + a, LEAF_DEV, stride=16), :].astype(BF16)
            total = total + dot(piece, spread_ref[a])
        moment_ref[:, c * COEF : (c + 1) * COEF] = total.astype(BF16)

    got_ref[...] = dot(pick_ref[...], moment_ref[...]).astype(BF16)
    for direction in range(9):
        residue = 8 - direction
        rows = slice(direction * 128, (direction + 1) * 128)
        grid = dot(place_ref[rows, :], got_ref[rows, :]).astype(BF16)
        steps = (OFFSETS - residue + 8) // 9
        left = jnp.concatenate(
            [
                jnp.concatenate(
                    [grid[o * ACT_MOST : (o + 1) * ACT_MOST, c * COEF : (c + 1) * COEF] for o in range(steps)], axis=1
                )
                for c in range(3)
            ],
            axis=0,
        )
        right = jnp.concatenate([ops_ref[residue + 9 * o] for o in range(steps)], axis=0)
        outs[direction // 3][direction % 3] = dot(left, right)


def source_features(raw):
    row = iota((8, LEAF_PART), 0)
    half = jnp.where(row < 3, raw * 0.5, 0.0)
    high = half.astype(BF16).astype(F32)
    low = (half - high).astype(BF16).astype(F32)
    near = high + low
    norm = jnp.sum(near * near, axis=0, keepdims=True)
    norm_high = norm.astype(BF16).astype(F32)
    rest = norm - norm_high
    norm_mid = rest.astype(BF16).astype(F32)
    norm_low = rest - norm_mid
    first = jnp.where(
        row < 3, high, jnp.where(row == 3, norm_high, jnp.where(row == 4, norm_mid, jnp.where(row == 5, norm_low, 1.0)))
    )
    second = jnp.where(row == 3, 1.0, low)
    return jnp.concatenate([first, second, high, low], axis=0).T.astype(BF16)


def target_features(raw, shift):
    row = iota((8, LEAF_PART), 0)
    moved = jnp.where(row < 3, raw * 0.5, 0.0) + shift
    high = moved.astype(BF16).astype(F32)
    low = (moved - high).astype(BF16).astype(F32)
    near = high + low
    norm = jnp.sum(near * near, axis=0, keepdims=True) + SMOOTH
    norm_high = norm.astype(BF16).astype(F32)
    rest = norm - norm_high
    norm_mid = rest.astype(BF16).astype(F32)
    norm_low = rest - norm_mid
    high = -2.0 * high
    low = -2.0 * low
    first = jnp.where(row < 3, high, jnp.where(row < 6, 1.0, jnp.where(row == 6, norm_high, norm_mid)))
    second = jnp.where(row == 3, norm_low, high)
    return jnp.concatenate([first, second, low, low], axis=0).astype(BF16)


def source_rows(raw):
    row = iota((8, LEAF_PART), 0)
    high = raw.astype(BF16).astype(F32)
    low = pltpu.roll(raw - high, 5, 0)
    return jnp.where(row < 3, low, jnp.where(row < 6, high, 0.0)).astype(BF16)


def leaf_rows(packet_ref, slot, base=0):
    return packet_ref[pl.ds(base + slot * ROWS_LEAF, 8), :]


def effect(target, source, shift):
    kernel = lax.rsqrt(dot(source_features(source), target_features(target, shift)))
    rows = source_rows(source)
    return dot(jnp.concatenate([rows, rows], axis=1), jnp.concatenate(split(kernel), axis=0))


def self_kernel(lists_ref, index_ref, packet_ref, shift_ref, total_ref):
    total_ref[...] = jnp.zeros_like(total_ref)
    count = index_ref[ACT_MOST]
    still = jnp.zeros((8, LEAF_PART), F32)
    group = 16

    def alone(step, carry):
        results = []
        for at in range(group):
            raw = leaf_rows(packet_ref, step * group + at)
            results.append(effect(raw, raw, still))
        for at in range(group):
            total_ref[step * group + at] = results[at]
        return carry

    lax.fori_loop(0, pl.cdiv(count, group), alone, 0)
    local_pairs(lists_ref, packet_ref, shift_ref, total_ref, 0, jnp.minimum(pl.cdiv(4 * count, PAIRS), FIRST))


def local_kernel(lists_ref, index_ref, packet_ref, shift_ref, near_ref, total_ref):
    total_ref[...] = near_ref[...]
    local_pairs(lists_ref, packet_ref, shift_ref, total_ref, FIRST, pl.cdiv(4 * index_ref[ACT_MOST], PAIRS))


def local_pairs(lists_ref, packet_ref, shift_ref, total_ref, begin, end):
    def pairs(step, carry):
        results = []
        for at in range(PAIRS):
            column = step * PAIRS + at
            first = lists_ref[0, column]
            second = lists_ref[1, column]
            code = lists_ref[2, column]
            one = leaf_rows(packet_ref, first)
            other = leaf_rows(packet_ref, second)
            results.append((first, effect(one, other, shift_ref[32 + code])))
            results.append((second, effect(other, one, shift_ref[code])))
        for slot, terms in results:
            total_ref[slot] += terms
        return carry

    lax.fori_loop(begin, end, pairs, 0)


def remote_kernel(
    lists_ref,
    index_ref,
    packet_ref,
    shift_ref,
    near_ref,
    before_ref,
    after_ref,
    lower_ref,
    upper_ref,
    block_ref,
    from_lower_ref,
    from_upper_ref,
    mix_ref,
    out_ref,
    total_ref,
    local_ref,
    meta_ref,
    got_ref,
    sem,
):
    back = ((after_ref, 2), (after_ref, 1), (after_ref, 0), (upper_ref, 0))
    front = ((before_ref, 0), (before_ref, 1), (before_ref, 2), (lower_ref, 0))
    for side, (ref, place) in enumerate(back):
        meta_ref[8 * side : 8 * side + 8, :] = ref[place * PACKET + META : place * PACKET + META + 8, :].astype(jnp.int32)
    copy = pltpu.make_async_copy(meta_ref, got_ref, sem)
    copy.start()
    total_ref[...] = near_ref[...]
    out_ref[...] = jnp.zeros_like(out_ref)
    middle = slice(3 * PACKET + 3 * ACT_MOST, 3 * PACKET + 6 * ACT_MOST)
    local_ref[...] = block_ref[1] + before_ref[middle, :] + after_ref[middle, :] + from_lower_ref[...] + from_upper_ref[...]

    def all_sides(sides, target_of, source_of, code_of, sign):
        def columns(step, carry):
            picks = []
            for side, (ref, place) in enumerate(sides):
                for at in range(PCAP // 4):
                    picks.append((side, ref, place, side * PCAP + step * (PCAP // 4) + at))
            targets = [target_of(side, column) for side, ref, place, column in picks]
            live = targets[0] != DEAD
            for target in targets[1:]:
                live = live | (target != DEAD)

            @pl.when(live)
            def _():
                results = []
                for target, (side, ref, place, column) in zip(targets, picks):
                    source = leaf_rows(ref, source_of(side, column), place * PACKET)
                    shift = shift_ref[sign + code_of(side, column)]
                    results.append(effect(leaf_rows(packet_ref, target), source, shift))
                for target, terms in zip(targets, results):
                    total_ref[target] += terms

            return carry

        lax.fori_loop(0, 4, columns, 0)

    all_sides(front, lambda side, c: lists_ref[3, c], lambda side, c: lists_ref[4, c], lambda side, c: lists_ref[5, c], 32)
    copy.wait()
    all_sides(
        back,
        lambda side, c: got_ref[8 * side + 1, c],
        lambda side, c: got_ref[8 * side, c],
        lambda side, c: got_ref[8 * side + 2, c],
        0,
    )

    count = index_ref[ACT_MOST]
    row = iota((8, GROUP_LEAVES * LEAF_PART), 0)

    def finish(step, carry):
        raw = jnp.concatenate([leaf_rows(packet_ref, step * GROUP_LEAVES + at) for at in range(GROUP_LEAVES)], axis=1)
        mixed = dot(mix_ref[...], features(jnp.where(row == 6, 1.0, raw)))
        high, low = split(mixed[0:COEF] * mixed[COEF : 2 * COEF] * mixed[2 * COEF :])
        results = []
        for at in range(GROUP_LEAVES):
            rows = [local_ref[pl.ds(c * ACT_MOST + step * GROUP_LEAVES + at, 1), :] for c in range(3)]
            left_high, left_low = split(jnp.concatenate(rows + [jnp.zeros((5, COEF), F32)], axis=0))
            part = slice(at * LEAF_PART, (at + 1) * LEAF_PART)
            far = dot(
                jnp.concatenate([left_high, left_high, left_low], axis=1),
                jnp.concatenate([high[:, part], low[:, part], high[:, part]], axis=0),
            )
            near = total_ref[step * GROUP_LEAVES + at]
            results.append((near + pltpu.roll(near, 5, 0) + far)[0:3])
        for at in range(GROUP_LEAVES):
            slot = step * GROUP_LEAVES + at

            @pl.when(slot < count)
            def _(at=at, slot=slot):
                here = pl.ds(pl.multiple_of(index_ref[slot] * LEAF_PART, LEAF_PART), LEAF_PART)
                out_ref[:, here] = results[at]

        return carry

    lax.fori_loop(0, pl.cdiv(count, GROUP_LEAVES), finish, 0)


def moved(value, axis, step):
    count = lax.axis_size(axis)
    first, last = (max(0, -step), min(count, count - step))
    return lax.ppermute(value, axis, [(source, source + step) for source in range(first, last)])


VMEM = pl.BlockSpec(memory_space=pltpu.VMEM)
SMEM = pl.BlockSpec(memory_space=pltpu.SMEM)


def on_device(positions, strengths, active, m2l_list, p2p_list, local_pairs, m2l_ops):
    far_list = m2l_list.reshape(27, 128)
    near_list = p2p_list.reshape(3, 128)
    pair_list = local_pairs.reshape(3, 128)
    params = pltpu.CompilerParams(vmem_limit_bytes=VMEM_LIMIT)
    shifts = jnp.asarray(displacements())

    packet, lists, index = pl.pallas_call(
        pack_kernel,
        out_shape=(
            jax.ShapeDtypeStruct((PACKET, 128), F32),
            jax.ShapeDtypeStruct((8, 128), jnp.int32),
            jax.ShapeDtypeStruct((64,), jnp.int32),
        ),
        in_specs=[SMEM] + [VMEM] * 6,
        out_specs=(VMEM, VMEM, SMEM),
        compiler_params=params,
        name="pack",
    )(active, positions, strengths, active.reshape(1, LEAF_DEV), far_list, near_list, pair_list)

    lower = moved(packet, "dev", 1)
    upper = moved(packet, "dev", -1)

    blocks_before, blocks, blocks_after = pl.pallas_call(
        far_kernel,
        out_shape=[jax.ShapeDtypeStruct((3, 3 * ACT_MOST, COEF), F32)] * 3,
        in_specs=[VMEM] * 6,
        out_specs=[VMEM] * 3,
        scratch_shapes=[
            pltpu.VMEM((LEAF_DEV * 16, 32), F32),
            pltpu.VMEM((LEAF_DEV, 3 * COEF), BF16),
            pltpu.VMEM((9 * 128, LEAF_DEV), BF16),
            pltpu.VMEM((9 * 128, 128), BF16),
            pltpu.VMEM((9 * 128, 3 * COEF), BF16),
        ],
        compiler_params=params,
        cost_estimate=pl.CostEstimate(flops=4_000_000_000, bytes_accessed=4_000_000, transcendentals=0),
        name="moments",
    )(positions, strengths, far_list, m2l_ops, jnp.asarray(moment_rows()), jnp.asarray(spreading()))

    three = [lower, packet, upper]
    to_upper = jnp.concatenate(three + [blocks_after.reshape(-1, 128)], axis=0)
    to_lower = jnp.concatenate(three + [blocks_before.reshape(-1, 128)], axis=0)
    before = moved(to_upper, "group", 1)
    after = moved(to_lower, "group", -1)

    total_shape = jax.ShapeDtypeStruct((ACT_MOST + 1, 8, LEAF_PART), F32)
    total = pl.pallas_call(
        self_kernel,
        out_shape=total_shape,
        in_specs=[SMEM, SMEM, VMEM, VMEM],
        out_specs=VMEM,
        compiler_params=params,
        cost_estimate=pl.CostEstimate(flops=4_000_000_000, bytes_accessed=4_000_000, transcendentals=0),
        name="self_pairs",
    )(lists, index, packet, shifts)
    before, after, total = lax.optimization_barrier((before, after, total))

    rows = 3 * ACT_MOST

    def summed(step):
        base = 3 * PACKET + step * rows
        return blocks[step] + before[base : base + rows] + after[base : base + rows]

    from_lower = moved(summed(2), "dev", 1)
    from_upper = moved(summed(0), "dev", -1)

    total = pl.pallas_call(
        local_kernel,
        out_shape=total_shape,
        in_specs=[SMEM, SMEM, VMEM, VMEM, VMEM],
        out_specs=VMEM,
        compiler_params=params,
        cost_estimate=pl.CostEstimate(flops=4_000_000_000, bytes_accessed=4_000_000, transcendentals=0),
        name="local_pairs",
    )(lists, index, packet, shifts, total)
    from_lower, from_upper, total = lax.optimization_barrier((from_lower, from_upper, total))

    return pl.pallas_call(
        remote_kernel,
        out_shape=jax.ShapeDtypeStruct(positions.shape, F32),
        in_specs=[SMEM, SMEM]
        + [VMEM] * 11,
        out_specs=VMEM,
        scratch_shapes=[
            pltpu.VMEM((ACT_MOST + 1, 8, LEAF_PART), F32),
            pltpu.VMEM((rows, COEF), F32),
            pltpu.VMEM((32, 128), jnp.int32),
            pltpu.SMEM((32, 128), jnp.int32),
            pltpu.SemaphoreType.DMA,
        ],
        compiler_params=params,
        cost_estimate=pl.CostEstimate(flops=4_000_000_000, bytes_accessed=4_000_000, transcendentals=0),
        name="remote_pairs",
    )(
        lists,
        index,
        packet,
        shifts,
        total,
        before,
        after,
        lower,
        upper,
        blocks,
        from_lower,
        from_upper,
        jnp.asarray(basis_rows()),
    )


def solution(mesh):
    in_specs = (
        P(None, ("group", "dev")),
        P(None, ("group", "dev")),
        P(("group", "dev")),
        P(("group", "dev"), None, None),
        P(("group", "dev"), None, None),
        P(("group", "dev"), None, None),
        P(),
    )
    out_specs = P(None, ("group", "dev"))
    return jax.shard_map(
        on_device, mesh=mesh, in_specs=in_specs, out_specs=out_specs, check_vma=False
    )
```

```python
import math

import jax
import jax.numpy as jnp
import ml_dtypes
import numpy as np
from jax import lax
from jax.experimental import pallas as pl
from jax.experimental.pallas import tpu as pltpu
from jax.sharding import PartitionSpec as P

COEF = 128
ORDER = 5
OFFSETS = 32
ACT_MOST = 32
LEAF_PART = 128
LEAF_DEV = 256
PCAP = 32
DEAD = ACT_MOST
ROWS_LEAF = 6
META = ROWS_LEAF * ACT_MOST
PACKET = META + 8
ROWS_FAR = 3 * ACT_MOST
GROUP_LEAVES = 8
PAIRS = 16
FIRST = 4
SMOOTH = 0.04
FORWARD_GROUP = (-1, -1, -1, 0)
FORWARD_MEMBER = (-1, 0, 1, -1)
VMEM_LIMIT = 56 * 1024 * 1024

F32 = jnp.float32
BF16 = jnp.bfloat16
NT = (((1,), (1,)), ((), ()))
NN = (((1,), (0,)), ((), ()))


def dot(left, right, dims=NN):
    return lax.dot_general(left, right, dims, preferred_element_type=F32)


def split(value):
    high = value.astype(BF16)
    return high, (value - high.astype(F32)).astype(BF16)


def iota(shape, dim):
    return lax.broadcasted_iota(jnp.int32, shape, dim)


def combination(rows):
    table = np.zeros((len(rows), 32), np.float64)
    for at, row in enumerate(rows):
        if row is None:
            continue
        raw, point = row
        if point is None:
            table[at, raw] = 1.0
            continue
        table[at, 6] = 1.0 / ORDER
        for degree in range(1, ORDER):
            angle = degree * (2 * point + 1) * math.pi / (2 * ORDER)
            table[at, 8 * (degree - 1) + raw] = 2.0 / ORDER * math.cos(angle)
    high = table.astype(ml_dtypes.bfloat16)
    low = (table - high.astype(np.float64)).astype(ml_dtypes.bfloat16)
    return np.concatenate([high, high, low], axis=1)


def moment_rows():
    points = range(ORDER)
    along_x = [(0, a) for c in range(3) for a in points] + [None]
    strength = [(3 + c, None) for c in range(3) for a in points] + [None]
    along_y = [(1, b) for b in points for g in points] + [None] * 7
    along_z = [(2, g) for b in points for g in points] + [None] * 7
    return combination(along_x + strength + along_y + along_z)


def basis_rows():
    points = range(ORDER)
    every = [(a, b, g) for a in points for b in points for g in points]
    return combination(
        [(dim, n[dim]) if n is not None else None for dim in range(3) for n in every + [None] * 3]
    )


def spreading():
    table = np.zeros((ORDER, 32, COEF), np.float32)
    for a in range(ORDER):
        for bg in range(ORDER**2):
            table[a, bg, a * ORDER**2 + bg] = 1.0
    return table.astype(ml_dtypes.bfloat16)


def displacements(shift_ref):
    row = iota((8, LEAF_PART), 0)
    for code in range(26):
        shifted = code + (1 if code >= 13 else 0)
        vector = (shifted // 9 - 1, shifted // 3 % 3 - 1, shifted % 3 - 1)
        value = jnp.zeros((8, LEAF_PART), F32)
        for dim in range(3):
            value = jnp.where(row == dim, float(vector[dim]), value)
        shift_ref[code] = value
        shift_ref[32 + code] = -value


def features(raw):
    second = 2.0 * raw * raw - 1.0
    third = 2.0 * raw * second - raw
    fourth = 2.0 * raw * third - second
    high, low = split(jnp.concatenate([raw, second, third, fourth], axis=0))
    return jnp.concatenate([high, low, high], axis=0)


def presence(targets, classes, residue):
    hit = (iota((LEAF_DEV, 128), 0) == targets).astype(F32).astype(BF16)
    counted = jnp.broadcast_to((classes == residue) & (targets >= 0), (16, 128))
    return dot(counted.astype(F32).astype(BF16), hit, NT).astype(BF16)


def below(targets):
    return (iota((LEAF_DEV, 128), 0) < targets).astype(F32).astype(BF16)


def front_kernel(
    flags_ref,
    active_ref,
    far_flat,
    near_flat,
    pairs_flat,
    mix_ref,
    spread_ref,
    pos_hbm,
    str_hbm,
    ops_hbm,
    to_upper_ref,
    to_lower_ref,
    stay_ref,
    lists_ref,
    index_ref,
    pos_ref,
    str_ref,
    ops_ref,
    cell_ref,
    moment_ref,
    pick_ref,
    place_ref,
    got_ref,
    left_ref,
    high_ref,
    low_ref,
    far_ref,
    near_ref,
    pairs_ref,
    sems,
):
    copies = [
        pltpu.make_async_copy(pos_hbm, pos_ref, sems.at[0]),
        pltpu.make_async_copy(str_hbm, str_ref, sems.at[1]),
        pltpu.make_async_copy(ops_hbm, ops_ref, sems.at[2]),
    ]
    for copy in copies:
        copy.start()
    for flat, ref, blocks in ((far_flat, far_ref, 9), (near_flat, near_ref, 1), (pairs_flat, pairs_ref, 1)):
        for kind in range(3):
            for block in range(blocks):
                row = kind * blocks + block
                ref[row : row + 1, :] = flat[kind, :, block * 128 : (block + 1) * 128]

    def enter(leaf, count):
        index_ref[count] = leaf
        return count + flags_ref[leaf]

    for slot in range(ACT_MOST):
        index_ref[slot] = 0
    count = lax.fori_loop(0, LEAF_DEV, enter, 0, unroll=16)
    index_ref[ACT_MOST] = count

    own = jnp.broadcast_to(active_ref[...].astype(F32), (16, LEAF_DEV)).astype(BF16)

    def own_slot(row):
        rank = dot(own, below(row))[0:1]
        return jnp.where(row >= 0, rank.astype(jnp.int32), DEAD)

    second = near_ref[1:2, :]
    under = below(second)
    lanes = iota((1, 128), 1)
    second_slot = jnp.full((1, 128), DEAD, jnp.int32)
    for side in range(4):
        direction = 3 * (FORWARD_GROUP[side] + 1) + FORWARD_MEMBER[side] + 1
        there = presence(
            far_ref[18 + direction : 19 + direction, :], far_ref[9 + direction : 10 + direction, :], 8 - direction
        )
        rank = dot(there, under)[0:1].astype(jnp.int32)
        mine = (lanes >= side * PCAP) & (lanes < (side + 1) * PCAP) & (second >= 0)
        second_slot = jnp.where(mine, rank, second_slot)
    first_slot = own_slot(near_ref[0:1, :])
    codes = near_ref[2:3, :]
    lists_ref[0:1, :] = own_slot(pairs_ref[0:1, :])
    lists_ref[1:2, :] = own_slot(pairs_ref[1:2, :])
    lists_ref[2:3, :] = pairs_ref[2:3, :]
    lists_ref[3:4, :] = first_slot
    lists_ref[4:5, :] = second_slot
    lists_ref[5:6, :] = codes
    lists_ref[6:8, :] = jnp.zeros((2, 128), jnp.int32)

    empty = jnp.zeros((7, 128), jnp.int32)
    classes = far_ref[9:18, :]
    targets = far_ref[18:27, :]
    residues = 8 - iota((9, 128), 0)
    counted = jnp.where((classes == residues) & (targets >= 0), targets, LEAF_DEV)
    counted = jnp.concatenate([counted, empty], axis=0).astype(F32).T
    sources = jnp.concatenate([far_ref[0:9, :], empty], axis=0).astype(F32).T
    leaves = iota((128, LEAF_DEV), 1).astype(F32)
    for direction in range(9):
        target = targets[direction : direction + 1]
        less = counted[:, direction : direction + 1] < target.astype(F32)
        rank = jnp.sum(jnp.where(less, 1.0, 0.0), axis=0, keepdims=True).astype(jnp.int32)
        kind = classes[direction : direction + 1]
        step = (kind >= 9).astype(jnp.int32) + (kind >= 18).astype(jnp.int32) + (kind >= 27).astype(jnp.int32)
        key = jnp.where(target >= 0, step * ACT_MOST + rank, -1)
        rows = slice(direction * 128, (direction + 1) * 128)
        place_ref[rows, :] = (iota((128, 128), 0) == key).astype(F32).astype(BF16)
        pick_ref[rows, :] = (sources[:, direction : direction + 1] == leaves).astype(F32).astype(BF16)

    copies[0].wait()
    copies[1].wait()
    for ref in (to_upper_ref, to_lower_ref):
        ref[META : META + 1, :] = first_slot.astype(F32)
        ref[META + 1 : META + 2, :] = second_slot.astype(F32)
        ref[META + 2 : META + 3, :] = codes.astype(F32)
        ref[META + 3 : PACKET, :] = jnp.zeros((5, 128), F32)
    for slot in range(ACT_MOST):
        leaf = jnp.where(slot < count, index_ref[slot], 0)
        here = pl.ds(pl.multiple_of(leaf * LEAF_PART, LEAF_PART), LEAF_PART)
        for ref in (to_upper_ref, to_lower_ref):
            ref[ROWS_LEAF * slot : ROWS_LEAF * slot + 3, :] = pos_ref[:, here]
            ref[ROWS_LEAF * slot + 3 : ROWS_LEAF * slot + 6, :] = str_ref[:, here]

    mix = mix_ref[...]
    width = GROUP_LEAVES * LEAF_PART
    lane_leaf = iota((32, 128), 1) // 16

    def parts(value):
        return [value[:, leaf * LEAF_PART : (leaf + 1) * LEAF_PART] for leaf in range(GROUP_LEAVES)]

    def expand(block, carry):
        here = pl.ds(pl.multiple_of(block * width, width), width)
        raw = jnp.concatenate(
            [pos_ref[:, here], str_ref[:, here], jnp.ones((1, width), F32), jnp.zeros((1, width), F32)], axis=0
        )
        mixed = dot(mix, features(raw))
        left_ref[pl.ds(pl.multiple_of(block * 128, 128), 128), :] = jnp.concatenate(parts(mixed[0:16] * mixed[16:32]), axis=0)
        right_high, right_low = split(mixed[32:64] * mixed[64:96])
        rows = pl.ds(pl.multiple_of(block * 256, 256), 256)
        high_ref[rows, :] = jnp.concatenate(parts(right_high), axis=0)
        low_ref[rows, :] = jnp.concatenate(parts(right_low), axis=0)
        return carry

    def contract(block, carry):
        left = left_ref[pl.ds(pl.multiple_of(block * 128, 128), 128), :].T
        left_high, left_low = split(left)
        rows = pl.ds(pl.multiple_of(block * 256, 256), 256)
        right_high = high_ref[rows, :]
        right_low = low_ref[rows, :]
        every = dot(
            jnp.concatenate([right_high, right_high, right_low], axis=1),
            jnp.concatenate([left_high, left_low, left_high], axis=0),
        )
        cells = every[0:32]
        for leaf in range(1, GROUP_LEAVES):
            cells = jnp.where(lane_leaf == leaf, every[32 * leaf : 32 * leaf + 32], cells)
        cell_ref[pl.ds(pl.multiple_of(block * 128, 128), 128), :] = cells.T
        return carry

    lax.fori_loop(0, LEAF_DEV // GROUP_LEAVES, expand, 0, unroll=8)
    lax.fori_loop(0, LEAF_DEV // GROUP_LEAVES, contract, 0, unroll=8)
    for c in range(3):
        total = jnp.zeros((LEAF_DEV, COEF), F32)
        for a in range(ORDER):
            piece = cell_ref[pl.ds(c * ORDER + a, LEAF_DEV, stride=16), :].astype(BF16)
            total = total + dot(piece, spread_ref[a])
        moment_ref[:, c * COEF : (c + 1) * COEF] = total.astype(BF16)

    copies[2].wait()
    got_ref[...] = dot(pick_ref[...], moment_ref[...]).astype(BF16)
    for direction in range(9):
        residue = 8 - direction
        rows = slice(direction * 128, (direction + 1) * 128)
        grid = dot(place_ref[rows, :], got_ref[rows, :]).astype(BF16)
        steps = (OFFSETS - residue + 8) // 9
        left = jnp.concatenate(
            [
                jnp.concatenate(
                    [grid[o * ACT_MOST : (o + 1) * ACT_MOST, c * COEF : (c + 1) * COEF] for o in range(steps)], axis=1
                )
                for c in range(3)
            ],
            axis=0,
        )
        right = jnp.concatenate([ops_ref[residue + 9 * o] for o in range(steps)], axis=0)
        along, across = direction // 3, direction % 3
        if across == 1:
            stay_ref[along] = dot(left, right)
        else:
            ref = to_lower_ref if across == 0 else to_upper_ref
            ref[PACKET + along * ROWS_FAR : PACKET + (along + 1) * ROWS_FAR, :] = dot(left, right)


def source_features(raw):
    row = iota((8, LEAF_PART), 0)
    half = jnp.where(row < 3, raw * 0.5, 0.0)
    high = half.astype(BF16).astype(F32)
    low = (half - high).astype(BF16).astype(F32)
    near = high + low
    norm = jnp.sum(near * near, axis=0, keepdims=True)
    norm_high = norm.astype(BF16).astype(F32)
    rest = norm - norm_high
    norm_mid = rest.astype(BF16).astype(F32)
    norm_low = rest - norm_mid
    first = jnp.where(
        row < 3, high, jnp.where(row == 3, norm_high, jnp.where(row == 4, norm_mid, jnp.where(row == 5, norm_low, 1.0)))
    )
    second = jnp.where(row == 3, 1.0, low)
    return jnp.concatenate([first, second, high, low], axis=0).T.astype(BF16)


def target_features(raw, shift):
    row = iota((8, LEAF_PART), 0)
    moved = jnp.where(row < 3, raw * 0.5, 0.0) + shift
    high = moved.astype(BF16).astype(F32)
    low = (moved - high).astype(BF16).astype(F32)
    near = high + low
    norm = jnp.sum(near * near, axis=0, keepdims=True) + SMOOTH
    norm_high = norm.astype(BF16).astype(F32)
    rest = norm - norm_high
    norm_mid = rest.astype(BF16).astype(F32)
    norm_low = rest - norm_mid
    high = -2.0 * high
    low = -2.0 * low
    first = jnp.where(row < 3, high, jnp.where(row < 6, 1.0, jnp.where(row == 6, norm_high, norm_mid)))
    second = jnp.where(row == 3, norm_low, high)
    return jnp.concatenate([first, second, low, low], axis=0).astype(BF16)


def source_rows(raw):
    row = iota((8, LEAF_PART), 0)
    high = raw.astype(BF16).astype(F32)
    low = pltpu.roll(raw - high, 5, 0)
    return jnp.where(row < 3, low, jnp.where(row < 6, high, 0.0)).astype(BF16)


def leaf_rows(packet_ref, slot, base=0):
    return packet_ref[pl.ds(base + slot * ROWS_LEAF, 8), :]


def effect(target, source, shift):
    kernel = lax.rsqrt(dot(source_features(source), target_features(target, shift)))
    rows = source_rows(source)
    return dot(jnp.concatenate([rows, rows], axis=1), jnp.concatenate(split(kernel), axis=0))


def self_kernel(lists_ref, index_ref, packet_ref, total_ref, shift_ref):
    displacements(shift_ref)
    total_ref[...] = jnp.zeros_like(total_ref)
    count = index_ref[ACT_MOST]
    still = jnp.zeros((8, LEAF_PART), F32)
    group = 16

    def alone(step, carry):
        results = []
        for at in range(group):
            raw = leaf_rows(packet_ref, step * group + at)
            results.append(effect(raw, raw, still))
        for at in range(group):
            total_ref[step * group + at] = results[at]
        return carry

    lax.fori_loop(0, pl.cdiv(count, group), alone, 0)
    local_pairs(lists_ref, packet_ref, shift_ref, total_ref, 0, jnp.minimum(pl.cdiv(4 * count, PAIRS), FIRST))


def local_kernel(lists_ref, index_ref, packet_ref, near_ref, total_ref, shift_ref):
    displacements(shift_ref)
    total_ref[...] = near_ref[...]
    local_pairs(lists_ref, packet_ref, shift_ref, total_ref, FIRST, pl.cdiv(4 * index_ref[ACT_MOST], PAIRS))


def local_pairs(lists_ref, packet_ref, shift_ref, total_ref, begin, end):
    def pairs(step, carry):
        results = []
        for at in range(PAIRS):
            column = step * PAIRS + at
            first = lists_ref[0, column]
            second = lists_ref[1, column]
            code = lists_ref[2, column]
            one = leaf_rows(packet_ref, first)
            other = leaf_rows(packet_ref, second)
            results.append((first, effect(one, other, shift_ref[32 + code])))
            results.append((second, effect(other, one, shift_ref[code])))
        for slot, terms in results:
            total_ref[slot] += terms
        return carry

    lax.fori_loop(begin, end, pairs, 0)


def relay_kernel(lower_ref, own_ref, upper_ref, stay_ref, to_after_ref, to_before_ref):
    for ref, along in ((to_after_ref, 2), (to_before_ref, 0)):
        for place, source in enumerate((lower_ref, own_ref, upper_ref)):
            ref[place * PACKET : (place + 1) * PACKET, :] = source[0:PACKET, :]
        rows = slice(PACKET + along * ROWS_FAR, PACKET + (along + 1) * ROWS_FAR)
        ref[3 * PACKET :, :] = stay_ref[along] + lower_ref[rows, :] + upper_ref[rows, :]


def remote_kernel(
    lists_ref,
    index_ref,
    packet_ref,
    near_ref,
    before_ref,
    after_ref,
    lower_ref,
    upper_ref,
    stay_ref,
    mix_ref,
    out_ref,
    total_ref,
    local_ref,
    shift_ref,
    meta_ref,
    got_ref,
    sem,
):
    back = ((after_ref, 2), (after_ref, 1), (after_ref, 0), (upper_ref, 0))
    front = ((before_ref, 0), (before_ref, 1), (before_ref, 2), (lower_ref, 0))
    for side, (ref, place) in enumerate(back):
        meta_ref[8 * side : 8 * side + 8, :] = ref[place * PACKET + META : place * PACKET + META + 8, :].astype(jnp.int32)
    copy = pltpu.make_async_copy(meta_ref, got_ref, sem)
    copy.start()
    displacements(shift_ref)
    total_ref[...] = near_ref[...]
    out_ref[...] = jnp.zeros_like(out_ref)
    rows = slice(PACKET + ROWS_FAR, PACKET + 2 * ROWS_FAR)
    local_ref[...] = (
        stay_ref[1] + lower_ref[rows, :] + upper_ref[rows, :] + before_ref[3 * PACKET :, :] + after_ref[3 * PACKET :, :]
    )

    def all_sides(sides, target_of, source_of, code_of, sign):
        def columns(step, carry):
            picks = []
            for side, (ref, place) in enumerate(sides):
                for at in range(PCAP // 4):
                    picks.append((side, ref, place, side * PCAP + step * (PCAP // 4) + at))
            targets = [target_of(side, column) for side, ref, place, column in picks]
            live = targets[0] != DEAD
            for target in targets[1:]:
                live = live | (target != DEAD)

            @pl.when(live)
            def _():
                results = []
                for target, (side, ref, place, column) in zip(targets, picks):
                    source = leaf_rows(ref, source_of(side, column), place * PACKET)
                    shift = shift_ref[sign + code_of(side, column)]
                    results.append(effect(leaf_rows(packet_ref, target), source, shift))
                for target, terms in zip(targets, results):
                    total_ref[target] += terms

            return carry

        lax.fori_loop(0, 4, columns, 0)

    all_sides(front, lambda side, c: lists_ref[3, c], lambda side, c: lists_ref[4, c], lambda side, c: lists_ref[5, c], 32)
    copy.wait()
    all_sides(
        back,
        lambda side, c: got_ref[8 * side + 1, c],
        lambda side, c: got_ref[8 * side, c],
        lambda side, c: got_ref[8 * side + 2, c],
        0,
    )

    count = index_ref[ACT_MOST]
    row = iota((8, GROUP_LEAVES * LEAF_PART), 0)

    def finish(step, carry):
        raw = jnp.concatenate([leaf_rows(packet_ref, step * GROUP_LEAVES + at) for at in range(GROUP_LEAVES)], axis=1)
        mixed = dot(mix_ref[...], features(jnp.where(row == 6, 1.0, raw)))
        high, low = split(mixed[0:COEF] * mixed[COEF : 2 * COEF] * mixed[2 * COEF :])
        results = []
        for at in range(GROUP_LEAVES):
            rows = [local_ref[pl.ds(c * ACT_MOST + step * GROUP_LEAVES + at, 1), :] for c in range(3)]
            left_high, left_low = split(jnp.concatenate(rows + [jnp.zeros((5, COEF), F32)], axis=0))
            part = slice(at * LEAF_PART, (at + 1) * LEAF_PART)
            far = dot(
                jnp.concatenate([left_high, left_high, left_low], axis=1),
                jnp.concatenate([high[:, part], low[:, part], high[:, part]], axis=0),
            )
            near = total_ref[step * GROUP_LEAVES + at]
            results.append((near + pltpu.roll(near, 5, 0) + far)[0:3])
        for at in range(GROUP_LEAVES):
            slot = step * GROUP_LEAVES + at

            @pl.when(slot < count)
            def _(at=at, slot=slot):
                here = pl.ds(pl.multiple_of(index_ref[slot] * LEAF_PART, LEAF_PART), LEAF_PART)
                out_ref[:, here] = results[at]

        return carry

    lax.fori_loop(0, pl.cdiv(count, GROUP_LEAVES), finish, 0)


def moved(value, axis, step):
    count = lax.axis_size(axis)
    first, last = (max(0, -step), min(count, count - step))
    return lax.ppermute(value, axis, [(source, source + step) for source in range(first, last)])


VMEM = pl.BlockSpec(memory_space=pltpu.VMEM)
SMEM = pl.BlockSpec(memory_space=pltpu.SMEM)
HBM = pl.BlockSpec(memory_space=pltpu.HBM)


def on_device(positions, strengths, active, m2l_list, p2p_list, local_pairs, m2l_ops):
    far_list = jnp.transpose(m2l_list, (1, 0, 2))
    near_list = jnp.transpose(p2p_list, (1, 0, 2))
    pair_list = jnp.transpose(local_pairs, (1, 0, 2))
    params = pltpu.CompilerParams(vmem_limit_bytes=VMEM_LIMIT)
    small = pltpu.CompilerParams(vmem_limit_bytes=16 * 1024 * 1024)
    shifts = pltpu.VMEM((64, 8, LEAF_PART), F32)

    leaf_columns = positions.shape[1]
    message = jax.ShapeDtypeStruct((PACKET + 3 * ROWS_FAR, 128), F32)
    to_upper, to_lower, stay, lists, index = pl.pallas_call(
        front_kernel,
        out_shape=(
            message,
            message,
            jax.ShapeDtypeStruct((3, ROWS_FAR, COEF), F32),
            jax.ShapeDtypeStruct((8, 128), jnp.int32),
            jax.ShapeDtypeStruct((64,), jnp.int32),
        ),
        in_specs=[SMEM] + [VMEM] * 6 + [HBM] * 3,
        out_specs=(VMEM, VMEM, VMEM, VMEM, SMEM),
        scratch_shapes=[
            pltpu.VMEM((3, leaf_columns), F32),
            pltpu.VMEM((3, leaf_columns), F32),
            pltpu.VMEM((OFFSETS, COEF, COEF), BF16),
            pltpu.VMEM((LEAF_DEV * 16, 32), F32),
            pltpu.VMEM((LEAF_DEV, 3 * COEF), BF16),
            pltpu.VMEM((9 * 128, LEAF_DEV), BF16),
            pltpu.VMEM((9 * 128, 128), BF16),
            pltpu.VMEM((9 * 128, 3 * COEF), BF16),
            pltpu.VMEM((LEAF_DEV * 16, LEAF_PART), F32),
            pltpu.VMEM((LEAF_DEV * 32, LEAF_PART), BF16),
            pltpu.VMEM((LEAF_DEV * 32, LEAF_PART), BF16),
            pltpu.VMEM((32, 128), jnp.int32),
            pltpu.VMEM((8, 128), jnp.int32),
            pltpu.VMEM((8, 128), jnp.int32),
            pltpu.SemaphoreType.DMA((3,)),
        ],
        compiler_params=params,
        name="front",
    )(
        active,
        active.reshape(1, LEAF_DEV),
        far_list,
        near_list,
        pair_list,
        jnp.asarray(moment_rows()),
        jnp.asarray(spreading()),
        positions,
        strengths,
        m2l_ops,
    )

    lower = moved(to_upper, "dev", 1)
    upper = moved(to_lower, "dev", -1)
    cost = pl.CostEstimate(flops=4_000_000_000, bytes_accessed=4_000_000, transcendentals=0)
    total_shape = jax.ShapeDtypeStruct((ACT_MOST + 1, 8, LEAF_PART), F32)
    total = pl.pallas_call(
        self_kernel,
        out_shape=total_shape,
        in_specs=[SMEM, SMEM, VMEM],
        out_specs=VMEM,
        scratch_shapes=[shifts],
        compiler_params=small,
        cost_estimate=cost,
        name="self_pairs",
    )(lists, index, to_upper)
    lower, upper, total = lax.optimization_barrier((lower, upper, total))

    relayed = jax.ShapeDtypeStruct((3 * PACKET + ROWS_FAR, 128), F32)
    to_after, to_before = pl.pallas_call(
        relay_kernel,
        out_shape=(relayed, relayed),
        in_specs=[VMEM] * 4,
        out_specs=(VMEM, VMEM),
        compiler_params=small,
        name="relay",
    )(lower, to_upper, upper, stay)
    before = moved(to_after, "group", 1)
    after = moved(to_before, "group", -1)

    total = pl.pallas_call(
        local_kernel,
        out_shape=total_shape,
        in_specs=[SMEM, SMEM, VMEM, VMEM],
        out_specs=VMEM,
        scratch_shapes=[shifts],
        compiler_params=small,
        cost_estimate=cost,
        name="local_pairs",
    )(lists, index, to_upper, total)
    before, after, total = lax.optimization_barrier((before, after, total))

    return pl.pallas_call(
        remote_kernel,
        out_shape=jax.ShapeDtypeStruct(positions.shape, F32),
        in_specs=[SMEM, SMEM] + [VMEM] * 8,
        out_specs=VMEM,
        scratch_shapes=[
            pltpu.VMEM((ACT_MOST + 1, 8, LEAF_PART), F32),
            pltpu.VMEM((ROWS_FAR, COEF), F32),
            shifts,
            pltpu.VMEM((32, 128), jnp.int32),
            pltpu.SMEM((32, 128), jnp.int32),
            pltpu.SemaphoreType.DMA,
        ],
        compiler_params=small,
        cost_estimate=cost,
        name="remote_pairs",
    )(lists, index, to_upper, total, before, after, lower, upper, stay, jnp.asarray(basis_rows()))


def solution(mesh):
    in_specs = (
        P(None, ("group", "dev")),
        P(None, ("group", "dev")),
        P(("group", "dev")),
        P(("group", "dev"), None, None),
        P(("group", "dev"), None, None),
        P(("group", "dev"), None, None),
        P(),
    )
    out_specs = P(None, ("group", "dev"))
    return jax.shard_map(
        on_device, mesh=mesh, in_specs=in_specs, out_specs=out_specs, check_vma=False
    )
```

```python
import math

import jax
import jax.numpy as jnp
import ml_dtypes
import numpy as np
from jax import lax
from jax.experimental import pallas as pl
from jax.experimental.pallas import tpu as pltpu
from jax.sharding import PartitionSpec as P

COEF = 128
ORDER = 5
OFFSETS = 32
ACT_MOST = 32
LEAF_PART = 128
LEAF_DEV = 256
PCAP = 32
DEAD = ACT_MOST
ROWS_LEAF = 6
META = ROWS_LEAF * ACT_MOST
PACKET = META + 8
ROWS_FAR = 3 * ACT_MOST
GROUP_LEAVES = 8
CHUNKS = 2
PAIRS = 32
SIDE = 16
FIRST = 1
SMOOTH = 0.04
FORWARD_GROUP = (-1, -1, -1, 0)
FORWARD_MEMBER = (-1, 0, 1, -1)
VMEM_LIMIT = 56 * 1024 * 1024

F32 = jnp.float32
BF16 = jnp.bfloat16
NT = (((1,), (1,)), ((), ()))
NN = (((1,), (0,)), ((), ()))


def dot(left, right, dims=NN):
    return lax.dot_general(left, right, dims, preferred_element_type=F32)


def split(value):
    high = value.astype(BF16)
    return high, (value - high.astype(F32)).astype(BF16)


def iota(shape, dim):
    return lax.broadcasted_iota(jnp.int32, shape, dim)


def combination(rows):
    table = np.zeros((len(rows), 32), np.float64)
    for at, row in enumerate(rows):
        if row is None:
            continue
        raw, point = row
        if point is None:
            table[at, raw] = 1.0
            continue
        table[at, 6] = 1.0 / ORDER
        for degree in range(1, ORDER):
            angle = degree * (2 * point + 1) * math.pi / (2 * ORDER)
            table[at, 8 * (degree - 1) + raw] = 2.0 / ORDER * math.cos(angle)
    high = table.astype(ml_dtypes.bfloat16)
    low = (table - high.astype(np.float64)).astype(ml_dtypes.bfloat16)
    return np.concatenate([high, high, low], axis=1)


def moment_rows():
    points = range(ORDER)
    along_x = [(0, a) for c in range(3) for a in points] + [None]
    strength = [(3 + c, None) for c in range(3) for a in points] + [None]
    along_y = [(1, b) for b in points for g in points] + [None] * 7
    along_z = [(2, g) for b in points for g in points] + [None] * 7
    return combination(along_x + strength + along_y + along_z)


def basis_rows():
    points = range(ORDER)
    every = [(a, b, g) for a in points for b in points for g in points]
    return combination(
        [(dim, n[dim]) if n is not None else None for dim in range(3) for n in every + [None] * 3]
    )


def spreading():
    table = np.zeros((ORDER, 32, COEF), np.float32)
    for a in range(ORDER):
        for bg in range(ORDER**2):
            table[a, bg, a * ORDER**2 + bg] = 1.0
    return table.astype(ml_dtypes.bfloat16)


def displacements(shift_ref):
    row = iota((8, LEAF_PART), 0)
    for code in range(26):
        shifted = code + (1 if code >= 13 else 0)
        vector = (shifted // 9 - 1, shifted // 3 % 3 - 1, shifted % 3 - 1)
        value = jnp.zeros((8, LEAF_PART), F32)
        for dim in range(3):
            value = jnp.where(row == dim, float(vector[dim]), value)
        shift_ref[code] = value
        shift_ref[32 + code] = -value


def features(raw):
    second = 2.0 * raw * raw - 1.0
    third = 2.0 * raw * second - raw
    fourth = 2.0 * raw * third - second
    high, low = split(jnp.concatenate([raw, second, third, fourth], axis=0))
    return jnp.concatenate([high, low, high], axis=0)


def presence(targets, classes, residue):
    hit = (iota((LEAF_DEV, 128), 0) == targets).astype(F32).astype(BF16)
    counted = jnp.broadcast_to((classes == residue) & (targets >= 0), (16, 128))
    return dot(counted.astype(F32).astype(BF16), hit, NT).astype(BF16)


def below(targets):
    return (iota((LEAF_DEV, 128), 0) < targets).astype(F32).astype(BF16)


def front_kernel(
    flags_ref,
    active_ref,
    far_flat,
    near_flat,
    pairs_flat,
    mix_ref,
    spread_ref,
    pos_hbm,
    str_hbm,
    ops_hbm,
    to_upper_ref,
    to_lower_ref,
    stay_ref,
    lists_ref,
    index_ref,
    pos_ref,
    str_ref,
    ops_ref,
    cell_ref,
    moment_ref,
    pick_ref,
    place_ref,
    got_ref,
    left_ref,
    high_ref,
    low_ref,
    far_ref,
    near_ref,
    pairs_ref,
    sems,
):
    span = pos_ref.shape[1] // CHUNKS

    def arriving(chunk):
        here = pl.ds(pl.multiple_of(chunk * span, span), span)
        return [
            pltpu.make_async_copy(pos_hbm.at[:, here], pos_ref.at[:, here], sems.at[chunk]),
            pltpu.make_async_copy(str_hbm.at[:, here], str_ref.at[:, here], sems.at[CHUNKS + chunk]),
        ]

    operators = [
        pltpu.make_async_copy(
            ops_hbm.at[part * 8 : part * 8 + 8], ops_ref.at[part * 8 : part * 8 + 8], sems.at[2 * CHUNKS + part]
        )
        for part in range(OFFSETS // 8)
    ]
    for copy in [copy for chunk in range(CHUNKS) for copy in arriving(chunk)] + operators:
        copy.start()
    for flat, ref, blocks in ((far_flat, far_ref, 9), (near_flat, near_ref, 1), (pairs_flat, pairs_ref, 1)):
        for kind in range(3):
            for block in range(blocks):
                row = kind * blocks + block
                ref[row : row + 1, :] = flat[kind, :, block * 128 : (block + 1) * 128]

    def enter(leaf, count):
        index_ref[count] = leaf
        return count + flags_ref[leaf]

    for slot in range(ACT_MOST):
        index_ref[slot] = 0
    count = lax.fori_loop(0, LEAF_DEV, enter, 0, unroll=16)
    index_ref[ACT_MOST] = count

    own = jnp.broadcast_to(active_ref[...].astype(F32), (16, LEAF_DEV)).astype(BF16)

    def own_slot(row):
        rank = dot(own, below(row))[0:1]
        return jnp.where(row >= 0, rank.astype(jnp.int32), DEAD)

    second = near_ref[1:2, :]
    under = below(second)
    lanes = iota((1, 128), 1)
    second_slot = jnp.full((1, 128), DEAD, jnp.int32)
    for side in range(4):
        direction = 3 * (FORWARD_GROUP[side] + 1) + FORWARD_MEMBER[side] + 1
        there = presence(
            far_ref[18 + direction : 19 + direction, :], far_ref[9 + direction : 10 + direction, :], 8 - direction
        )
        rank = dot(there, under)[0:1].astype(jnp.int32)
        mine = (lanes >= side * PCAP) & (lanes < (side + 1) * PCAP) & (second >= 0)
        second_slot = jnp.where(mine, rank, second_slot)
    first_slot = own_slot(near_ref[0:1, :])
    codes = near_ref[2:3, :]
    lists_ref[0:1, :] = own_slot(pairs_ref[0:1, :])
    lists_ref[1:2, :] = own_slot(pairs_ref[1:2, :])
    lists_ref[2:3, :] = pairs_ref[2:3, :]
    lists_ref[3:4, :] = first_slot
    lists_ref[4:5, :] = second_slot
    lists_ref[5:6, :] = codes
    lists_ref[6:8, :] = jnp.zeros((2, 128), jnp.int32)

    empty = jnp.zeros((7, 128), jnp.int32)
    classes = far_ref[9:18, :]
    targets = far_ref[18:27, :]
    residues = 8 - iota((9, 128), 0)
    counted = jnp.where((classes == residues) & (targets >= 0), targets, LEAF_DEV)
    counted = jnp.concatenate([counted, empty], axis=0).astype(F32).T
    sources = jnp.concatenate([far_ref[0:9, :], empty], axis=0).astype(F32).T
    leaves = iota((128, LEAF_DEV), 1).astype(F32)
    for direction in range(9):
        target = targets[direction : direction + 1]
        less = counted[:, direction : direction + 1] < target.astype(F32)
        rank = jnp.sum(jnp.where(less, 1.0, 0.0), axis=0, keepdims=True).astype(jnp.int32)
        kind = classes[direction : direction + 1]
        step = (kind >= 9).astype(jnp.int32) + (kind >= 18).astype(jnp.int32) + (kind >= 27).astype(jnp.int32)
        key = jnp.where(target >= 0, step * ACT_MOST + rank, -1)
        rows = slice(direction * 128, (direction + 1) * 128)
        place_ref[rows, :] = (iota((128, 128), 0) == key).astype(F32).astype(BF16)
        pick_ref[rows, :] = (sources[:, direction : direction + 1] == leaves).astype(F32).astype(BF16)

    mix = mix_ref[...]
    width = GROUP_LEAVES * LEAF_PART
    lane_leaf = iota((32, 128), 1) // 16

    def parts(value):
        return [value[:, leaf * LEAF_PART : (leaf + 1) * LEAF_PART] for leaf in range(GROUP_LEAVES)]

    def expand(block, carry):
        here = pl.ds(pl.multiple_of(block * width, width), width)
        raw = jnp.concatenate(
            [pos_ref[:, here], str_ref[:, here], jnp.ones((1, width), F32), jnp.zeros((1, width), F32)], axis=0
        )
        mixed = dot(mix, features(raw))
        left_ref[pl.ds(pl.multiple_of(block * 128, 128), 128), :] = jnp.concatenate(parts(mixed[0:16] * mixed[16:32]), axis=0)
        right_high, right_low = split(mixed[32:64] * mixed[64:96])
        rows = pl.ds(pl.multiple_of(block * 256, 256), 256)
        high_ref[rows, :] = jnp.concatenate(parts(right_high), axis=0)
        low_ref[rows, :] = jnp.concatenate(parts(right_low), axis=0)
        return carry

    def contract(block, carry):
        left = left_ref[pl.ds(pl.multiple_of(block * 128, 128), 128), :].T
        left_high, left_low = split(left)
        rows = pl.ds(pl.multiple_of(block * 256, 256), 256)
        right_high = high_ref[rows, :]
        right_low = low_ref[rows, :]
        every = dot(
            jnp.concatenate([right_high, right_high, right_low], axis=1),
            jnp.concatenate([left_high, left_low, left_high], axis=0),
        )
        cells = every[0:32]
        for leaf in range(1, GROUP_LEAVES):
            cells = jnp.where(lane_leaf == leaf, every[32 * leaf : 32 * leaf + 32], cells)
        cell_ref[pl.ds(pl.multiple_of(block * 128, 128), 128), :] = cells.T
        return carry

    blocks = LEAF_DEV // GROUP_LEAVES // CHUNKS

    def expand_chunk(chunk, carry):
        for copy in arriving(chunk):
            copy.wait()
        for block in range(blocks):
            expand(chunk * blocks + block, carry)
        return carry

    lax.fori_loop(0, CHUNKS, expand_chunk, 0)
    for ref in (to_upper_ref, to_lower_ref):
        ref[META : META + 1, :] = first_slot.astype(F32)
        ref[META + 1 : META + 2, :] = second_slot.astype(F32)
        ref[META + 2 : META + 3, :] = codes.astype(F32)
        ref[META + 3 : PACKET, :] = jnp.zeros((5, 128), F32)
    for slot in range(ACT_MOST):
        leaf = jnp.where(slot < count, index_ref[slot], 0)
        here = pl.ds(pl.multiple_of(leaf * LEAF_PART, LEAF_PART), LEAF_PART)
        for ref in (to_upper_ref, to_lower_ref):
            ref[ROWS_LEAF * slot : ROWS_LEAF * slot + 3, :] = pos_ref[:, here]
            ref[ROWS_LEAF * slot + 3 : ROWS_LEAF * slot + 6, :] = str_ref[:, here]

    lax.fori_loop(0, LEAF_DEV // GROUP_LEAVES, contract, 0, unroll=16)
    for c in range(3):
        total = jnp.zeros((LEAF_DEV, COEF), F32)
        for a in range(ORDER):
            piece = cell_ref[pl.ds(c * ORDER + a, LEAF_DEV, stride=16), :].astype(BF16)
            total = total + dot(piece, spread_ref[a])
        moment_ref[:, c * COEF : (c + 1) * COEF] = total.astype(BF16)

    for copy in operators:
        copy.wait()
    got_ref[...] = dot(pick_ref[...], moment_ref[...]).astype(BF16)
    for direction in range(9):
        residue = 8 - direction
        rows = slice(direction * 128, (direction + 1) * 128)
        grid = dot(place_ref[rows, :], got_ref[rows, :]).astype(BF16)
        steps = (OFFSETS - residue + 8) // 9
        left = jnp.concatenate(
            [
                jnp.concatenate(
                    [grid[o * ACT_MOST : (o + 1) * ACT_MOST, c * COEF : (c + 1) * COEF] for o in range(steps)], axis=1
                )
                for c in range(3)
            ],
            axis=0,
        )
        right = jnp.concatenate([ops_ref[residue + 9 * o] for o in range(steps)], axis=0)
        along, across = direction // 3, direction % 3
        if across == 1:
            stay_ref[along] = dot(left, right)
        else:
            ref = to_lower_ref if across == 0 else to_upper_ref
            ref[PACKET + along * ROWS_FAR : PACKET + (along + 1) * ROWS_FAR, :] = dot(left, right)


def source_features(raw):
    row = iota((8, LEAF_PART), 0)
    half = jnp.where(row < 3, raw * 0.5, 0.0)
    high = half.astype(BF16).astype(F32)
    low = (half - high).astype(BF16).astype(F32)
    near = high + low
    norm = jnp.sum(near * near, axis=0, keepdims=True)
    norm_high = norm.astype(BF16).astype(F32)
    rest = norm - norm_high
    norm_mid = rest.astype(BF16).astype(F32)
    norm_low = rest - norm_mid
    first = jnp.where(
        row < 3, high, jnp.where(row == 3, norm_high, jnp.where(row == 4, norm_mid, jnp.where(row == 5, norm_low, 1.0)))
    )
    second = jnp.where(row == 3, 1.0, low)
    return jnp.concatenate([first, second, high, low], axis=0)


def target_features(raw, shift):
    row = iota((8, LEAF_PART), 0)
    moved = jnp.where(row < 3, raw * 0.5, 0.0) + shift
    high = moved.astype(BF16).astype(F32)
    low = (moved - high).astype(BF16).astype(F32)
    near = high + low
    norm = jnp.sum(near * near, axis=0, keepdims=True) + SMOOTH
    norm_high = norm.astype(BF16).astype(F32)
    rest = norm - norm_high
    norm_mid = rest.astype(BF16).astype(F32)
    norm_low = rest - norm_mid
    high = -2.0 * high
    low = -2.0 * low
    first = jnp.where(row < 3, high, jnp.where(row < 6, 1.0, jnp.where(row == 6, norm_high, norm_mid)))
    second = jnp.where(row == 3, norm_low, high)
    return jnp.concatenate([first, second, low, low], axis=0).astype(BF16)


def source_rows(raw):
    row = iota((8, LEAF_PART), 0)
    high = raw.astype(BF16).astype(F32)
    low = pltpu.roll(raw - high, 5, 0)
    return jnp.where(row < 3, low, jnp.where(row < 6, high, 0.0)).astype(BF16)


def leaf_rows(packet_ref, slot, base=0):
    return packet_ref[pl.ds(base + slot * ROWS_LEAF, 8), :]


def effects(parts):
    results = []
    nothing = jnp.zeros((32, LEAF_PART), BF16)
    for at in range(0, len(parts), 2):
        (target, source, shift), (target_too, source_too, shift_too) = parts[at : at + 2]
        sources = jnp.concatenate([source_features(source), source_features(source_too)], axis=0).T.astype(BF16)
        targets = jnp.concatenate(
            [
                jnp.concatenate([target_features(target, shift), nothing], axis=1),
                jnp.concatenate([nothing, target_features(target_too, shift_too)], axis=1),
            ],
            axis=0,
        )
        kernel = jnp.concatenate(split(lax.rsqrt(dot(sources, targets))), axis=0)
        rows = jnp.concatenate([source_rows(source), source_rows(source_too)], axis=0)
        terms = dot(jnp.concatenate([rows, rows], axis=1), kernel)
        results += [terms[0:8, 0:LEAF_PART], terms[8:16, LEAF_PART:]]
    return results


def self_kernel(lists_ref, index_ref, message_hbm, total_ref, packet_ref, shift_ref, sem):
    copy = pltpu.make_async_copy(message_hbm.at[0:PACKET], packet_ref, sem)
    copy.start()
    displacements(shift_ref)
    total_ref[...] = jnp.zeros_like(total_ref)
    still = jnp.zeros((8, LEAF_PART), F32)
    copy.wait()
    raws = [leaf_rows(packet_ref, slot) for slot in range(ACT_MOST)]
    for slot, terms in enumerate(effects([(raw, raw, still) for raw in raws])):
        total_ref[slot] = terms
    end = jnp.minimum(pl.cdiv(4 * index_ref[ACT_MOST], PAIRS), FIRST)
    local_pairs(lists_ref, packet_ref, shift_ref, total_ref, 0, end)


def local_kernel(lists_ref, index_ref, packet_ref, near_ref, total_ref, shift_ref):
    displacements(shift_ref)
    total_ref[...] = near_ref[...]
    local_pairs(lists_ref, packet_ref, shift_ref, total_ref, FIRST, pl.cdiv(4 * index_ref[ACT_MOST], PAIRS))


def local_pairs(lists_ref, packet_ref, shift_ref, total_ref, begin, end):
    def pairs(step, carry):
        slots, parts = [], []
        for at in range(PAIRS):
            column = step * PAIRS + at
            first = lists_ref[0, column]
            second = lists_ref[1, column]
            code = lists_ref[2, column]
            one = leaf_rows(packet_ref, first)
            other = leaf_rows(packet_ref, second)
            slots += [first, second]
            parts += [(one, other, shift_ref[32 + code]), (other, one, shift_ref[code])]
        for slot, terms in zip(slots, effects(parts)):
            total_ref[slot] += terms
        return carry

    lax.fori_loop(begin, end, pairs, 0)


def relay_kernel(lower_ref, own_ref, upper_ref, stay_ref, to_after_ref, to_before_ref):
    for ref, along in ((to_after_ref, 2), (to_before_ref, 0)):
        for place, source in enumerate((lower_ref, own_ref, upper_ref)):
            ref[place * PACKET : (place + 1) * PACKET, :] = source[0:PACKET, :]
        rows = slice(PACKET + along * ROWS_FAR, PACKET + (along + 1) * ROWS_FAR)
        ref[3 * PACKET :, :] = stay_ref[along] + lower_ref[rows, :] + upper_ref[rows, :]


def remote_kernel(
    lists_ref,
    index_ref,
    packet_ref,
    near_ref,
    before_ref,
    after_ref,
    lower_ref,
    upper_ref,
    stay_ref,
    mix_ref,
    out_ref,
    total_ref,
    local_ref,
    shift_ref,
    meta_ref,
    got_ref,
    sem,
):
    back = ((after_ref, 2), (after_ref, 1), (after_ref, 0), (upper_ref, 0))
    front = ((before_ref, 0), (before_ref, 1), (before_ref, 2), (lower_ref, 0))
    for side, (ref, place) in enumerate(back):
        meta_ref[8 * side : 8 * side + 8, :] = ref[place * PACKET + META : place * PACKET + META + 8, :].astype(jnp.int32)
    copy = pltpu.make_async_copy(meta_ref, got_ref, sem)
    copy.start()
    displacements(shift_ref)
    total_ref[...] = near_ref[...]
    out_ref[...] = jnp.zeros_like(out_ref)
    rows = slice(PACKET + ROWS_FAR, PACKET + 2 * ROWS_FAR)
    local_ref[...] = (
        stay_ref[1] + lower_ref[rows, :] + upper_ref[rows, :] + before_ref[3 * PACKET :, :] + after_ref[3 * PACKET :, :]
    )

    def all_sides(sides, target_of, source_of, code_of, sign):
        def columns(step, carry):
            picks = []
            for side, (ref, place) in enumerate(sides):
                for at in range(SIDE):
                    picks.append((side, ref, place, side * PCAP + step * SIDE + at))
            targets = [target_of(side, column) for side, ref, place, column in picks]
            live = targets[0] != DEAD
            for target in targets[1:]:
                live = live | (target != DEAD)

            @pl.when(live)
            def _():
                parts = []
                for target, (side, ref, place, column) in zip(targets, picks):
                    source = leaf_rows(ref, source_of(side, column), place * PACKET)
                    shift = shift_ref[sign + code_of(side, column)]
                    parts.append((leaf_rows(packet_ref, target), source, shift))
                for target, terms in zip(targets, effects(parts)):
                    total_ref[target] += terms

            return carry

        lax.fori_loop(0, PCAP // SIDE, columns, 0)

    all_sides(front, lambda side, c: lists_ref[3, c], lambda side, c: lists_ref[4, c], lambda side, c: lists_ref[5, c], 32)
    copy.wait()
    all_sides(
        back,
        lambda side, c: got_ref[8 * side + 1, c],
        lambda side, c: got_ref[8 * side, c],
        lambda side, c: got_ref[8 * side + 2, c],
        0,
    )

    count = index_ref[ACT_MOST]
    row = iota((8, GROUP_LEAVES * LEAF_PART), 0)

    def finish(step, carry):
        raw = jnp.concatenate([leaf_rows(packet_ref, step * GROUP_LEAVES + at) for at in range(GROUP_LEAVES)], axis=1)
        mixed = dot(mix_ref[...], features(jnp.where(row == 6, 1.0, raw)))
        high, low = split(mixed[0:COEF] * mixed[COEF : 2 * COEF] * mixed[2 * COEF :])
        results = []
        for at in range(GROUP_LEAVES):
            rows = [local_ref[pl.ds(c * ACT_MOST + step * GROUP_LEAVES + at, 1), :] for c in range(3)]
            left_high, left_low = split(jnp.concatenate(rows + [jnp.zeros((5, COEF), F32)], axis=0))
            part = slice(at * LEAF_PART, (at + 1) * LEAF_PART)
            far = dot(
                jnp.concatenate([left_high, left_high, left_low], axis=1),
                jnp.concatenate([high[:, part], low[:, part], high[:, part]], axis=0),
            )
            near = total_ref[step * GROUP_LEAVES + at]
            results.append((near + pltpu.roll(near, 5, 0) + far)[0:3])
        for at in range(GROUP_LEAVES):
            slot = step * GROUP_LEAVES + at

            @pl.when(slot < count)
            def _(at=at, slot=slot):
                here = pl.ds(pl.multiple_of(index_ref[slot] * LEAF_PART, LEAF_PART), LEAF_PART)
                out_ref[:, here] = results[at]

        return carry

    lax.fori_loop(0, pl.cdiv(count, GROUP_LEAVES), finish, 0)


def moved(value, axis, step):
    count = lax.axis_size(axis)
    first, last = (max(0, -step), min(count, count - step))
    return lax.ppermute(value, axis, [(source, source + step) for source in range(first, last)])


VMEM = pl.BlockSpec(memory_space=pltpu.VMEM)
SMEM = pl.BlockSpec(memory_space=pltpu.SMEM)
HBM = pl.BlockSpec(memory_space=pltpu.HBM)


def on_device(positions, strengths, active, m2l_list, p2p_list, local_pairs, m2l_ops):
    far_list = jnp.transpose(m2l_list, (1, 0, 2))
    near_list = jnp.transpose(p2p_list, (1, 0, 2))
    pair_list = jnp.transpose(local_pairs, (1, 0, 2))
    params = pltpu.CompilerParams(vmem_limit_bytes=VMEM_LIMIT)
    small = pltpu.CompilerParams(vmem_limit_bytes=16 * 1024 * 1024)
    shifts = pltpu.VMEM((64, 8, LEAF_PART), F32)

    leaf_columns = positions.shape[1]
    message = jax.ShapeDtypeStruct((PACKET + 3 * ROWS_FAR, 128), F32)
    to_upper, to_lower, stay, lists, index = pl.pallas_call(
        front_kernel,
        out_shape=(
            message,
            message,
            jax.ShapeDtypeStruct((3, ROWS_FAR, COEF), F32),
            jax.ShapeDtypeStruct((8, 128), jnp.int32),
            jax.ShapeDtypeStruct((64,), jnp.int32),
        ),
        in_specs=[SMEM] + [VMEM] * 6 + [HBM] * 3,
        out_specs=(VMEM, VMEM, VMEM, VMEM, SMEM),
        scratch_shapes=[
            pltpu.VMEM((3, leaf_columns), F32),
            pltpu.VMEM((3, leaf_columns), F32),
            pltpu.VMEM((OFFSETS, COEF, COEF), BF16),
            pltpu.VMEM((LEAF_DEV * 16, 32), F32),
            pltpu.VMEM((LEAF_DEV, 3 * COEF), BF16),
            pltpu.VMEM((9 * 128, LEAF_DEV), BF16),
            pltpu.VMEM((9 * 128, 128), BF16),
            pltpu.VMEM((9 * 128, 3 * COEF), BF16),
            pltpu.VMEM((LEAF_DEV * 16, LEAF_PART), F32),
            pltpu.VMEM((LEAF_DEV * 32, LEAF_PART), BF16),
            pltpu.VMEM((LEAF_DEV * 32, LEAF_PART), BF16),
            pltpu.VMEM((32, 128), jnp.int32),
            pltpu.VMEM((8, 128), jnp.int32),
            pltpu.VMEM((8, 128), jnp.int32),
            pltpu.SemaphoreType.DMA((2 * CHUNKS + OFFSETS // 8,)),
        ],
        compiler_params=params,
        name="front",
    )(
        active,
        active.reshape(1, LEAF_DEV),
        far_list,
        near_list,
        pair_list,
        jnp.asarray(moment_rows()),
        jnp.asarray(spreading()),
        positions,
        strengths,
        m2l_ops,
    )

    lower = moved(to_upper, "dev", 1)
    upper = moved(to_lower, "dev", -1)
    cost = pl.CostEstimate(flops=4_000_000_000, bytes_accessed=4_000_000, transcendentals=0)
    total_shape = jax.ShapeDtypeStruct((ACT_MOST + 1, 8, LEAF_PART), F32)
    total = pl.pallas_call(
        self_kernel,
        out_shape=total_shape,
        in_specs=[SMEM, SMEM, HBM],
        out_specs=VMEM,
        scratch_shapes=[pltpu.VMEM((PACKET, 128), F32), shifts, pltpu.SemaphoreType.DMA],
        compiler_params=params,
        cost_estimate=cost,
        name="self_pairs",
    )(lists, index, to_upper)
    lower, upper, total = lax.optimization_barrier((lower, upper, total))

    relayed = jax.ShapeDtypeStruct((3 * PACKET + ROWS_FAR, 128), F32)
    to_after, to_before = pl.pallas_call(
        relay_kernel,
        out_shape=(relayed, relayed),
        in_specs=[VMEM] * 4,
        out_specs=(VMEM, VMEM),
        compiler_params=small,
        name="relay",
    )(lower, to_upper, upper, stay)
    before = moved(to_after, "group", 1)
    after = moved(to_before, "group", -1)

    total = pl.pallas_call(
        local_kernel,
        out_shape=total_shape,
        in_specs=[SMEM, SMEM, VMEM, VMEM],
        out_specs=VMEM,
        scratch_shapes=[shifts],
        compiler_params=small,
        cost_estimate=cost,
        name="local_pairs",
    )(lists, index, to_upper, total)
    before, after, total = lax.optimization_barrier((before, after, total))

    return pl.pallas_call(
        remote_kernel,
        out_shape=jax.ShapeDtypeStruct(positions.shape, F32),
        in_specs=[SMEM, SMEM] + [VMEM] * 8,
        out_specs=VMEM,
        scratch_shapes=[
            pltpu.VMEM((ACT_MOST + 1, 8, LEAF_PART), F32),
            pltpu.VMEM((ROWS_FAR, COEF), F32),
            shifts,
            pltpu.VMEM((32, 128), jnp.int32),
            pltpu.SMEM((32, 128), jnp.int32),
            pltpu.SemaphoreType.DMA,
        ],
        compiler_params=small,
        cost_estimate=cost,
        name="remote_pairs",
    )(lists, index, to_upper, total, before, after, lower, upper, stay, jnp.asarray(basis_rows()))


def solution(mesh):
    in_specs = (
        P(None, ("group", "dev")),
        P(None, ("group", "dev")),
        P(("group", "dev")),
        P(("group", "dev"), None, None),
        P(("group", "dev"), None, None),
        P(("group", "dev"), None, None),
        P(),
    )
    out_specs = P(None, ("group", "dev"))
    return jax.shard_map(
        on_device, mesh=mesh, in_specs=in_specs, out_specs=out_specs, check_vma=False
    )
```
